256 devices in a mesh: row: 8 (over z), lm: 32 (over x, y, core).
Axes of the slice: x: 4, y: 4, z: 8, core: 2. Of those that a mesh axis runs over, the one named last changes fastest.
Arguments:
- fingerprints: int32 [4096, 2048], P('row'), may hold values from 0 to 7, as said below
- landmarks: int32 [16384, 2048], P('lm'), may hold values from 0 to 7, as said below
- whitening: bfloat16 [16384, 512], P('lm'), may hold values from -0.046875 to 0.046875
- memberships: int32 [4096], P('row'), may hold values from 0 to 4095
Outputs:
- centroids: float32 [4096, 512], P('row', 'lm')
The draws below stay inside these ranges and needn't reach their ends.
Inputs may be any that keep to these rules, and one draw needn't show every extreme that they name: `fingerprints`: entries are counts; every row has at least one nonzero entry. `landmarks`: entries are counts; every row has at least one nonzero entry.
All inputs are finite; a program needn't handle non-finite values.
Results may differ from the reference program's by a relative error of at most 0.0025.
Values sent between devices are 32-bit elements; how exact they have to be, the bound alone decides.
No kernel may reach another device: no remote copies, remote signals or barrier semaphores. Data moves between devices by JAX's collectives and lax.ppermute only.
A program may use at most 64 MiB of HBM per device.

```python
import jax
import jax.numpy as jnp
from jax import lax

F = 2048
LEVELS = 7
LANDMARKS = 16384
FEAT = 512
CENT = 4096
ROWS = 4096


def count_rows(key, total_rows):
    keys = jax.random.split(key, 4)
    density = jax.random.randint(keys[0], (total_rows, 1), 1, 9)
    keep = jax.random.randint(keys[1], (total_rows, F), 0, 16) < density
    values = jax.random.randint(keys[2], (total_rows, F), 1, LEVELS + 1)
    marked = jax.random.randint(keys[3], (total_rows, 1), 0, F)
    columns = jnp.arange(F, dtype=jnp.int32)[None, :]
    counts = jnp.where(keep, values, 0)
    return jnp.where(columns == marked, values, counts).astype(jnp.int32)


def draw_fingerprints(key, part):
    key = jax.random.fold_in(key, 11)
    return count_rows(key, ROWS)


def draw_landmarks(key, part):
    key = jax.random.fold_in(key, 23)
    return count_rows(key, LANDMARKS)


def with_ends(result, key, smallest, high):
    longest = result.shape.index(max(result.shape))
    spots = []
    for shift in (0, 1):
        where = [jax.random.randint(jax.random.fold_in(key, axis), (), 0, length) for axis, length in enumerate(result.shape)]
        where[longest] = (where[longest] + shift) % result.shape[longest]
        spots.append(tuple(where))
    return result.at[spots[0]].set(smallest).at[spots[1]].set(high)


def shard_levels(key, dims, shards, smallest, high):
    def one(position, shards_of):
        heights = jax.random.uniform(jax.random.fold_in(jax.random.fold_in(key, 6), position), (shards_of,), jnp.float32, smallest / len(shards), high / len(shards))
        return jnp.repeat(jnp.exp(heights), dims[position] // shards_of).reshape((-1,) + (1,) * (len(dims) - position - 1))

    loudness = one(*shards[0])
    for cut in shards[1:]:
        loudness = loudness * one(*cut)
    return loudness


def scatter_about(own_key, dims, scale, reach, cuts=(), held_as=jnp.bfloat16):
    array = scale * jax.random.normal(own_key, dims, jnp.float32)
    if cuts:
        array = array * shard_levels(own_key, dims, cuts, -0.22, 0.18)
    return jnp.clip(array, -reach, reach).astype(held_as)


def setup_inputs(seed: int = 0) -> dict:
    key_of = jax.random.split(jax.random.key(seed), 5)
    return {
        "fingerprints": draw_fingerprints(jax.random.fold_in(key_of[4], 71), 0),
        "landmarks": draw_landmarks(jax.random.fold_in(key_of[4], 71), 0),
        "whitening": scatter_about(key_of[2], (LANDMARKS, FEAT), LANDMARKS ** -0.5, 0.046875, ((0, 32),)),
        "memberships": with_ends(jax.random.randint(key_of[3], (ROWS,), 0, CENT), jax.random.fold_in(key_of[3], 1), 0, CENT - 1).astype(jnp.int32),
    }


def shared_counts(rows, lands):
    total = jnp.zeros((rows.shape[0], lands.shape[0]), jnp.float32)
    for level in range(1, LEVELS + 1):
        left = (rows >= level).astype(jnp.float32)
        right = (lands >= level).astype(jnp.float32)
        total = total + jnp.dot(left, right.T, preferred_element_type=jnp.float32, precision=lax.Precision.HIGHEST)
    return total

def reference(fingerprints, landmarks, whitening, memberships):
    shared = shared_counts(fingerprints, landmarks)
    row_total = lax.optimization_barrier(jnp.sum(fingerprints, axis=1)).astype(jnp.float32)
    land_total = lax.optimization_barrier(jnp.sum(landmarks, axis=1)).astype(jnp.float32)
    kernel = (shared / (row_total[:, None] + land_total[None, :] - shared)).astype(jnp.bfloat16)
    raw = jnp.dot(kernel, whitening, preferred_element_type=jnp.float32)
    features = raw / jnp.sqrt(lax.optimization_barrier(jnp.mean(raw * raw, axis=1, keepdims=True)) + 1e-06)
    sums = jax.ops.segment_sum(features, memberships, num_segments=CENT)
    counts = jax.ops.segment_sum(jnp.ones(memberships.shape, jnp.float32), memberships, num_segments=CENT)
    return sums / jnp.maximum(counts, 1.0)[:, None]
```

```python
import functools

import jax
import jax.numpy as jnp
from jax import lax
from jax.experimental import pallas as pl
from jax.experimental.pallas import tpu as pltpu
from jax.sharding import PartitionSpec as P

LEVELS = 7
F8 = jnp.float8_e4m3fn
CHUNKS = (512, 512, 512, 512)
MIB = 1 << 20


def dot_nt(left, right):
    return lax.dot_general(left, right, (((1,), (1,)), ((), ())), preferred_element_type=jnp.float32)


def partial_features(half_ref, fp, lm, w, other, own, fp_v, lm_v, w_v, shared, row_total, land_total, sem):
    copies, at = [], 0
    for i, width in enumerate(CHUNKS):
        where = (slice(None), pl.ds(at, width))
        pair = (
            pltpu.make_async_copy(fp.at[where], fp_v.at[where], sem.at[2 * i]),
            pltpu.make_async_copy(lm.at[where], lm_v.at[where], sem.at[2 * i + 1]),
        )
        for copy in pair:
            copy.start()
        copies.append(pair)
        at += width
    w_copy = pltpu.make_async_copy(w, w_v, sem.at[2 * len(CHUNKS)])
    w_copy.start()
    one, zero = jnp.ones((), jnp.bfloat16), jnp.zeros((), jnp.bfloat16)
    at = 0
    for i, width in enumerate(CHUNKS):
        for copy in copies[i]:
            copy.wait()
        a = fp_v[:, at : at + width].astype(jnp.float32).astype(jnp.bfloat16)
        b = lm_v[:, at : at + width].astype(jnp.float32).astype(jnp.bfloat16)
        at += width
        rows = jnp.sum(a.astype(jnp.float32), axis=1, keepdims=True)
        lands = dot_nt(jnp.ones((8, width), jnp.bfloat16), b)[:1]
        left, right = [], []
        for level in range(1, LEVELS + 1):
            t = jnp.bfloat16(level)
            left.append((a if level == LEVELS else jnp.minimum(a, t)).astype(F8))
            right.append(jnp.where(b == t, one, zero).astype(F8))
        part = dot_nt(jnp.concatenate(left, 1), jnp.concatenate(right, 1))
        if i == 0:
            shared[...], row_total[...], land_total[...] = part, rows, lands
        else:
            shared[...] += part
            row_total[...] += rows
            land_total[...] += lands
    w_copy.wait()
    half = shared.shape[0] // 2
    mine = half_ref[0]
    for out, which in ((other, 1 - mine), (own, mine)):
        rows = pl.ds(pl.multiple_of(which * half, half), half)
        s = shared[rows, :]
        kernel = (s / (row_total[rows, :] + land_total[...] - s)).astype(jnp.bfloat16)
        out[...] = jnp.dot(kernel, w_v[...], preferred_element_type=jnp.float32)


def normalise(parts, out, turned):
    raw = parts[0]
    for i in range(1, parts.shape[0]):
        raw = raw + parts[i]
    rows, feat = raw.shape
    features = raw / jnp.sqrt(jnp.mean(raw * raw, axis=1, keepdims=True) + 1e-06)
    padded = jnp.concatenate([features, jnp.zeros((128 - rows, feat), jnp.float32)], 0)
    turned[...] = padded.T
    owners = feat // 16
    copies = out.shape[0] // (2 * owners)
    for h in range(2):
        block = jnp.concatenate(
            [turned[pl.ds(8 * h + f, owners, stride=16), :][:, :rows] for f in range(8)], 1
        )
        for z in range(copies):
            out[pl.ds(2 * owners * z + h, owners, stride=2), :] = block


def centroid_update(blocks, member, first_ref, out, *turned):
    sources, rows = member.shape
    cents = out.shape[1]
    for h in range(2):
        columns = blocks[pl.ds(h, sources, stride=2), :].T
        for part, ref in enumerate(turned):
            ref[pl.ds(128 * h, 128), :] = columns[:, 128 * part : 128 * (part + 1)]
    label = lax.broadcasted_iota(jnp.int32, (sources, cents), 1)
    local = member[...] - first_ref[0]
    acc = jnp.zeros((64, cents), jnp.float32)
    for j in range(rows):
        value = jnp.concatenate([ref[pl.ds(j, 16, stride=16), :] for ref in turned], 1)
        high = value.astype(jnp.bfloat16)
        rest = value - high.astype(jnp.float32)
        mid = rest.astype(jnp.bfloat16)
        low = (rest - mid.astype(jnp.float32)).astype(jnp.bfloat16)
        left = jnp.concatenate([high, mid, low, jnp.ones((16, sources), jnp.bfloat16)], 0)
        onehot = jnp.where(local[:, j : j + 1] == label, 1.0, 0.0).astype(jnp.bfloat16)
        acc = acc + jnp.dot(left, onehot, preferred_element_type=jnp.float32)
    sums = acc[0:16] + (acc[16:32] + acc[32:48])
    out[...] = sums / jnp.maximum(acc[48:49], 1.0)


def on_device(fingerprints, landmarks, whitening, memberships):
    rows, width = fingerprints.shape
    lands, feat = whitening.shape
    n_row, n_lm = lax.axis_size("row"), lax.axis_size("lm")
    chips = n_lm // 2
    owned = rows // n_lm
    half = rows // 2
    core = lax.axis_index("lm") % 2
    hbm, vmem, smem = (
        pl.BlockSpec(memory_space=m) for m in (pltpu.HBM, pltpu.VMEM, pltpu.SMEM)
    )
    other, own = pl.pallas_call(
        partial_features,
        in_specs=[smem, hbm, hbm, hbm],
        out_specs=[vmem, vmem],
        out_shape=[jax.ShapeDtypeStruct((half, feat), jnp.float32)] * 2,
        scratch_shapes=[
            pltpu.VMEM((rows, width), jnp.int32),
            pltpu.VMEM((lands, width), jnp.int32),
            pltpu.VMEM((lands, feat), jnp.bfloat16),
            pltpu.VMEM((rows, lands), jnp.float32),
            pltpu.VMEM((rows, 1), jnp.float32),
            pltpu.VMEM((1, lands), jnp.float32),
            pltpu.SemaphoreType.DMA((2 * len(CHUNKS) + 1,)),
        ],
        compiler_params=pltpu.CompilerParams(vmem_limit_bytes=60 * MIB),
        name="partial_features",
    )(core[None].astype(jnp.int32), fingerprints, landmarks, whitening)

    theirs = lax.ppermute(other, "lm", [(i, i ^ 1) for i in range(n_lm)])
    both = own + theirs
    parts = lax.all_to_all(
        both, "lm", 0, 0, tiled=True,
        axis_index_groups=[[2 * q + k for q in range(chips)] for k in range(2)],
    )

    spread = jnp.broadcast_to(memberships.reshape(1, -1, 128), (n_row, rows // 128, 128))
    member = lax.all_to_all(spread, "row", 0, 0, tiled=True)
    member = member.reshape(n_row, 2, chips, owned).transpose(0, 2, 1, 3).reshape(n_row * n_lm, owned)

    blocks = pl.pallas_call(
        normalise,
        in_specs=[vmem],
        out_specs=vmem,
        out_shape=jax.ShapeDtypeStruct((n_row * n_lm * 2, 128), jnp.float32),
        scratch_shapes=[pltpu.VMEM((feat, 128), jnp.float32)],
        name="normalise",
    )(parts.reshape(chips, owned, feat))
    blocks = lax.all_to_all(blocks, ("row", "lm"), 0, 0, tiled=True)

    cents = 4096 // n_row
    first = (lax.axis_index("row") * cents)[None].astype(jnp.int32)
    out = pl.pallas_call(
        centroid_update,
        in_specs=[vmem, vmem, smem],
        out_specs=vmem,
        out_shape=jax.ShapeDtypeStruct((feat // n_lm, cents), jnp.float32),
        scratch_shapes=[pltpu.VMEM((256, 128), jnp.float32)] * (n_row * n_lm // 128),
        name="centroid_update",
    )(blocks, member, first)
    return out.T


def solution(mesh):
    in_specs = (P("row", None), P("lm", None), P("lm", None), P("row"))
    out_specs = P("row", "lm")
    return jax.shard_map(
        on_device, mesh=mesh, in_specs=in_specs, out_specs=out_specs, check_vma=False
    )
```

```python
import jax
import jax.numpy as jnp
from jax import lax
from jax.experimental import pallas as pl
from jax.experimental.pallas import tpu as pltpu
from jax.sharding import Mesh
from jax.sharding import PartitionSpec as P

LEVELS = 7
F8 = jnp.float8_e4m3fn
CHUNKS = (128, 128, 256, 512, 512, 512)
MIB = 1 << 20


def dot_nt(left, right):
    return lax.dot_general(left, right, (((1,), (1,)), ((), ())), preferred_element_type=jnp.float32)


def partial_features(half_ref, fp, lm, w, other, own, fp_v, lm_v, w_v, shared, row_total, land_total, *rest):
    factors, sem = (rest[0:2], rest[2:4]), rest[4]
    copies, starts, at = [], [], 0
    for i, width in enumerate(CHUNKS):
        where = (slice(None), pl.ds(at, width))
        pair = (
            pltpu.make_async_copy(fp.at[where], fp_v.at[where], sem.at[2 * i]),
            pltpu.make_async_copy(lm.at[where], lm_v.at[where], sem.at[2 * i + 1]),
        )
        for copy in pair:
            copy.start()
        copies.append(pair)
        starts.append(at)
        at += width
    w_copy = pltpu.make_async_copy(w, w_v, sem.at[2 * len(CHUNKS)])
    w_copy.start()
    one, zero = jnp.ones((), jnp.bfloat16), jnp.zeros((), jnp.bfloat16)

    def convert(i):
        width, (left, right) = CHUNKS[i], factors[i % 2]
        for copy in copies[i]:
            copy.wait()
        a = fp_v[:, starts[i] : starts[i] + width].astype(jnp.float32)
        b = lm_v[:, starts[i] : starts[i] + width].astype(jnp.float32).astype(jnp.bfloat16)
        rows = jnp.sum(a, axis=1, keepdims=True)
        lands = dot_nt(jnp.ones((8, width), jnp.bfloat16), b)[:1]
        if i == 0:
            row_total[...], land_total[...] = rows, lands
        else:
            row_total[...] += rows
            land_total[...] += lands
        a = a.astype(jnp.bfloat16)
        for level in range(1, LEVELS + 1):
            t = jnp.bfloat16(level)
            where = slice((level - 1) * width, level * width)
            left[:, where] = (a if level == LEVELS else jnp.minimum(a, t)).astype(F8)
            right[:, where] = jnp.where(b == t, one, zero).astype(F8)

    convert(0)
    for i, width in enumerate(CHUNKS):
        left, right = factors[i % 2]
        part = dot_nt(left[:, : LEVELS * width], right[:, : LEVELS * width])
        if i == 0:
            shared[...] = part
        else:
            shared[...] += part
        if i + 1 < len(CHUNKS):
            convert(i + 1)
    w_copy.wait()
    half = shared.shape[0] // 2
    mine = half_ref[0]
    for which in (1 - mine, mine):
        rows = pl.ds(pl.multiple_of(which * half, half), half)
        s = shared[rows, :]
        kernel = (s / (row_total[rows, :] + land_total[...] - s)).astype(jnp.bfloat16)
        out = own if which is mine else other
        out[...] = jnp.dot(kernel, w_v[...], preferred_element_type=jnp.float32)


def add_theirs(own, theirs, both):
    both[...] = own[...] + theirs[...]


def normalise(place_ref, parts, member, out, turned):
    raw = parts[0]
    for i in range(1, parts.shape[0]):
        raw = raw + parts[i]
    rows, feat = raw.shape
    features = raw / jnp.sqrt(jnp.mean(raw * raw, axis=1, keepdims=True) + 1e-06)
    padded = jnp.concatenate([features, jnp.zeros((128 - rows, feat), jnp.float32)], 0)
    turned[...] = padded.T
    owners = feat // 16
    copies = out.shape[0] // (3 * owners)
    line = member[pl.ds(place_ref[0], 1), :].astype(jnp.float32)
    line = pltpu.roll(line, 128 - rows * place_ref[1], axis=1)
    line = jnp.broadcast_to(line, (owners, 128))
    for h in range(3):
        block = line
        if h < 2:
            block = jnp.concatenate(
                [turned[pl.ds(8 * h + f, owners, stride=16), :][:, :rows] for f in range(8)], 1
            )
        for z in range(copies):
            out[pl.ds(3 * owners * z + h, owners, stride=3), :] = block


def centroid_update(blocks, first_ref, out, *turned):
    sources, rows, cents = blocks.shape[0] // 3, 16, out.shape[1]
    for h in range(2):
        columns = blocks[pl.ds(h, sources, stride=3), :].T
        for part, ref in enumerate(turned):
            ref[pl.ds(128 * h, 128), :] = columns[:, 128 * part : 128 * (part + 1)]
    label = lax.broadcasted_iota(jnp.int32, (sources, cents), 1)
    local = blocks[pl.ds(2, sources, stride=3), :].astype(jnp.int32) - first_ref[0]
    acc = jnp.zeros((64, cents), jnp.float32)
    for j in range(rows):
        value = jnp.concatenate([ref[pl.ds(j, 16, stride=16), :] for ref in turned], 1)
        high = value.astype(jnp.bfloat16)
        rest = value - high.astype(jnp.float32)
        mid = rest.astype(jnp.bfloat16)
        low = (rest - mid.astype(jnp.float32)).astype(jnp.bfloat16)
        left = jnp.concatenate([high, mid, low, jnp.ones((16, sources), jnp.bfloat16)], 0)
        onehot = jnp.where(local[:, j : j + 1] == label, 1.0, 0.0).astype(jnp.bfloat16)
        acc = acc + jnp.dot(left, onehot, preferred_element_type=jnp.float32)
    sums = acc[0:16] + (acc[16:32] + acc[32:48])
    out[...] = sums / jnp.maximum(acc[48:49], 1.0)


def on_device(fingerprints, landmarks, whitening, memberships):
    rows, width = fingerprints.shape
    lands, feat = whitening.shape
    n_row, chips, cores = (lax.axis_size(a) for a in ("row", "chip", "core"))
    n_lm = chips * cores
    owned = rows // n_lm
    half = rows // 2
    core = lax.axis_index("core").astype(jnp.int32)
    hbm, vmem, smem = (
        pl.BlockSpec(memory_space=m) for m in (pltpu.HBM, pltpu.VMEM, pltpu.SMEM)
    )
    factor = pltpu.VMEM((rows, LEVELS * max(CHUNKS)), F8)
    small = pltpu.CompilerParams(vmem_limit_bytes=12 * MIB)
    other, own = pl.pallas_call(
        partial_features,
        in_specs=[smem, hbm, hbm, hbm],
        out_specs=[vmem, vmem],
        out_shape=[jax.ShapeDtypeStruct((half, feat), jnp.float32)] * 2,
        scratch_shapes=[
            pltpu.VMEM((rows, width), jnp.int32),
            pltpu.VMEM((lands, width), jnp.int32),
            pltpu.VMEM((lands, feat), jnp.bfloat16),
            pltpu.VMEM((rows, lands), jnp.float32),
            pltpu.VMEM((rows, 1), jnp.float32),
            pltpu.VMEM((1, lands), jnp.float32),
            factor, factor, factor, factor,
            pltpu.SemaphoreType.DMA((2 * len(CHUNKS) + 1,)),
        ],
        compiler_params=pltpu.CompilerParams(vmem_limit_bytes=57 * MIB),
        name="partial_features",
    )(core[None], fingerprints, landmarks, whitening)

    theirs = lax.ppermute(other, "core", [(0, 1), (1, 0)])
    both = pl.pallas_call(
        add_theirs,
        in_specs=[vmem] * 2,
        out_specs=vmem,
        out_shape=jax.ShapeDtypeStruct((half, feat), jnp.float32),
        compiler_params=small,
        name="add_theirs",
    )(own, theirs)
    parts = lax.all_to_all(both, "chip", 0, 0, tiled=True)

    chip = lax.axis_index("chip").astype(jnp.int32)
    each = 128 // owned
    place = jnp.stack([core * (half // 128) + chip // each, chip % each])
    blocks = pl.pallas_call(
        normalise,
        in_specs=[smem, vmem, vmem],
        out_specs=vmem,
        out_shape=jax.ShapeDtypeStruct((n_row * n_lm * 3, 128), jnp.float32),
        scratch_shapes=[pltpu.VMEM((feat, 128), jnp.float32)],
        compiler_params=small,
        name="normalise",
    )(place, parts.reshape(chips, owned, feat), memberships.reshape(-1, 128))
    blocks = lax.all_to_all(
        blocks.reshape(n_row * n_lm, 1, 3 * 128), ("row", "chip", "core"), 0, 0, tiled=True
    ).reshape(-1, 128)

    cents = 4096 // n_row
    first = (lax.axis_index("row") * cents)[None].astype(jnp.int32)
    out = pl.pallas_call(
        centroid_update,
        in_specs=[vmem, smem],
        out_specs=vmem,
        out_shape=jax.ShapeDtypeStruct((feat // n_lm, cents), jnp.float32),
        scratch_shapes=[pltpu.VMEM((256, 128), jnp.float32)] * (n_row * n_lm // 128),
        compiler_params=small,
        name="centroid_update",
    )(blocks, first)
    return out.T


def solution(mesh):
    lm = ("chip", "core")
    inner = Mesh(mesh.devices.reshape(mesh.shape["row"], -1, 2), ("row",) + lm)
    in_specs = (P("row", None), P(lm, None), P(lm, None), P("row"))
    out_specs = P("row", lm)
    return jax.shard_map(
        on_device, mesh=inner, in_specs=in_specs, out_specs=out_specs, check_vma=False
    )
```

```python
import functools

import jax
import jax.numpy as jnp
from jax import lax
from jax.experimental import pallas as pl
from jax.experimental.pallas import tpu as pltpu
from jax.sharding import Mesh
from jax.sharding import PartitionSpec as P

LEVELS = 7
F8 = jnp.float8_e4m3fn
CHUNKS = (128, 128, 256, 512, 512, 512)
MIB = 1 << 20


def dot_nt(left, right):
    return lax.dot_general(left, right, (((1,), (1,)), ((), ())), preferred_element_type=jnp.float32)


def partial_features(fp, lm, w, other, own, fp_v, lm_v, w_v, turned_w, shared, row_total, land_total, *rest):
    factors, sem = (rest[0:2], rest[2:4]), rest[4]
    w_copy = pltpu.make_async_copy(w, w_v, sem.at[2 * len(CHUNKS)])
    w_copy.start()
    copies, starts, at = [], [], 0
    for i, width in enumerate(CHUNKS):
        where = (slice(None), pl.ds(at, width))
        pair = (
            pltpu.make_async_copy(fp.at[where], fp_v.at[where], sem.at[2 * i]),
            pltpu.make_async_copy(lm.at[where], lm_v.at[where], sem.at[2 * i + 1]),
        )
        for copy in pair:
            copy.start()
        copies.append(pair)
        starts.append(at)
        at += width
    one, zero = jnp.ones((), jnp.bfloat16), jnp.zeros((), jnp.bfloat16)

    feat = w_v.shape[1]
    half = feat // 2
    column = lax.broadcasted_iota(jnp.int32, (feat, half), 0)
    place = lax.broadcasted_iota(jnp.int32, (feat, half), 1)
    place = 2 * (place - place % 16) + place % 16
    this = lax.axis_index("core")
    w_copy.wait()
    for part, core in enumerate((1 - this, this)):
        pick = jnp.where(column == place + 16 * core, 1.0, 0.0).astype(jnp.bfloat16)
        picked = jnp.dot(w_v[...], pick, preferred_element_type=jnp.float32)
        turned_w[:, part * half : (part + 1) * half] = picked.astype(jnp.bfloat16)

    def convert(i):
        width, (left, right) = CHUNKS[i], factors[i % 2]
        for copy in copies[i]:
            copy.wait()
        a = fp_v[:, starts[i] : starts[i] + width].astype(jnp.float32)
        b = lm_v[:, starts[i] : starts[i] + width].astype(jnp.float32).astype(jnp.bfloat16)
        rows = jnp.sum(a, axis=1, keepdims=True)
        lands = dot_nt(jnp.ones((8, width), jnp.bfloat16), b)[:1]
        if i == 0:
            row_total[...], land_total[...] = rows, lands
        else:
            row_total[...] += rows
            land_total[...] += lands
        a = a.astype(jnp.bfloat16)
        for level in range(1, LEVELS + 1):
            t = jnp.bfloat16(level)
            where = slice((level - 1) * width, level * width)
            left[:, where] = (a if level == LEVELS else jnp.minimum(a, t)).astype(F8)
            right[:, where] = jnp.where(b == t, one, zero).astype(F8)

    convert(0)
    for i, width in enumerate(CHUNKS):
        left, right = factors[i % 2]
        part = dot_nt(left[:, : LEVELS * width], right[:, : LEVELS * width])
        if i == 0:
            shared[...] = part
        else:
            shared[...] += part
        if i + 1 < len(CHUNKS):
            convert(i + 1)
    step = 256
    for at in range(0, shared.shape[0], step):
        rows = pl.ds(at, step)
        s = shared[rows, :]
        kernel = (s / (row_total[rows, :] + land_total[...] - s)).astype(jnp.bfloat16)
        raw = jnp.dot(kernel, turned_w[...], preferred_element_type=jnp.float32)
        other[rows, :], own[rows, :] = raw[:, :half], raw[:, half:]


def add_theirs(own, theirs, both):
    both[...] = own[...] + theirs[...]


def sum_parts(parts, turned, squares):
    raw = parts[0]
    for i in range(1, parts.shape[0]):
        raw = raw + parts[i]
    rows, half = raw.shape
    raw = jnp.concatenate([raw, jnp.zeros((128 - rows, half), jnp.float32)], 0).T
    turned[...] = raw
    squares[...] = jnp.broadcast_to(jnp.sum(raw * raw, axis=0, keepdims=True), squares.shape)


def lay_out(turned, member, lines):
    owners = turned.shape[0] // 16
    rows, count = 128 // 4, lines.shape[0] - 1
    for h in range(count):
        lines[h] = jnp.concatenate(
            [turned[pl.ds(4 * h + f, owners, stride=16), :][:, :rows] for f in range(4)], 1
        )
    chip = lax.axis_index("chip")
    line = member[pl.ds(chip // 4, 1), :].astype(jnp.float32)
    line = pltpu.roll(line, 128 - rows * (chip % 4), axis=1)
    lines[count] = jnp.broadcast_to(line, (owners, 128))


def normalise(lines, mine, theirs, out, *, feat):
    count, owners, _ = lines.shape
    rows = 128 // 4
    root = jnp.sqrt((mine[...] + theirs[...])[:1] / feat + 1e-06)
    root = jnp.concatenate([root[:, :rows]] * 4, 1)
    for h in range(count):
        line = lines[h] / root if h + 1 < count else lines[h]
        for z in range(out.shape[0] // (count * owners)):
            out[pl.ds(count * owners * z + h, owners, stride=count), :] = line


def centroid_update(blocks, out, turned):
    count, rows, cents = 5, 32, out.shape[1]
    sources = blocks.shape[0] // count
    for h in range(count - 1):
        turned[pl.ds(128 * h, 128), :] = blocks[pl.ds(h, sources, stride=count), :].T
    label = lax.broadcasted_iota(jnp.int32, (sources, cents), 1)
    local = blocks[pl.ds(count - 1, sources, stride=count), :].astype(jnp.int32) - lax.axis_index("row") * cents
    acc = jnp.zeros((64, cents), jnp.float32)
    for j in range(0, rows, 2):
        both = (j, j + 1)
        value = jnp.concatenate([turned[pl.ds(i, 16, stride=rows), :] for i in both], 1)
        high = value.astype(jnp.bfloat16)
        rest = value - high.astype(jnp.float32)
        mid = rest.astype(jnp.bfloat16)
        low = (rest - mid.astype(jnp.float32)).astype(jnp.bfloat16)
        left = jnp.concatenate([high, mid, low, jnp.ones((16, 2 * sources), jnp.bfloat16)], 0)
        onehot = jnp.concatenate(
            [jnp.where(local[:, i : i + 1] == label, 1.0, 0.0).astype(jnp.bfloat16) for i in both], 0
        )
        acc = acc + jnp.dot(left, onehot, preferred_element_type=jnp.float32)
    sums = acc[0:16] + (acc[16:32] + acc[32:48])
    out[...] = sums / jnp.maximum(acc[48:49], 1.0)


def on_device(fingerprints, landmarks, whitening, memberships):
    rows, width = fingerprints.shape
    lands, feat = whitening.shape
    n_row, chips, cores = (lax.axis_size(a) for a in ("row", "chip", "core"))
    half = feat // cores
    owned = rows // chips
    sources, lines = n_row * chips, 5
    hbm, vmem = (pl.BlockSpec(memory_space=m) for m in (pltpu.HBM, pltpu.VMEM))
    factor = pltpu.VMEM((rows, LEVELS * max(CHUNKS)), F8)
    small = pltpu.CompilerParams(vmem_limit_bytes=12 * MIB)

    def f32(*shape):
        return jax.ShapeDtypeStruct(shape, jnp.float32)

    other, own = pl.pallas_call(
        partial_features,
        in_specs=[hbm] * 3,
        out_specs=[vmem, vmem],
        out_shape=[f32(rows, half)] * 2,
        scratch_shapes=[
            pltpu.VMEM((rows, width), jnp.int32),
            pltpu.VMEM((lands, width), jnp.int32),
            pltpu.VMEM((lands, feat), jnp.bfloat16),
            pltpu.VMEM((lands, feat), jnp.bfloat16),
            pltpu.VMEM((rows, lands), jnp.float32),
            pltpu.VMEM((rows, 1), jnp.float32),
            pltpu.VMEM((1, lands), jnp.float32),
            factor, factor, factor, factor,
            pltpu.SemaphoreType.DMA((2 * len(CHUNKS) + 1,)),
        ],
        compiler_params=pltpu.CompilerParams(vmem_limit_bytes=40 * MIB),
        name="partial_features",
    )(
        *(pltpu.with_memory_space_constraint(x, pltpu.HBM) for x in (fingerprints, landmarks, whitening)),
    )

    theirs = lax.ppermute(other, "core", [(0, 1), (1, 0)])
    both = pl.pallas_call(
        add_theirs,
        in_specs=[vmem] * 2,
        out_specs=vmem,
        out_shape=f32(rows, half),
        compiler_params=small,
        name="add_theirs",
    )(own, theirs)
    parts = lax.all_to_all(both, "chip", 0, 0, tiled=True)

    turned, squares = pl.pallas_call(
        sum_parts,
        in_specs=[vmem],
        out_specs=[vmem] * 2,
        out_shape=[f32(half, 128), f32(8, 128)],
        compiler_params=small,
        name="sum_parts",
    )(parts.reshape(chips, owned, half))
    their_squares = lax.ppermute(squares, "core", [(0, 1), (1, 0)])
    blocks = pl.pallas_call(
        lay_out,
        in_specs=[vmem] * 2,
        out_specs=vmem,
        out_shape=f32(lines, chips, 128),
        compiler_params=small,
        name="lay_out",
    )(turned, pltpu.with_memory_space_constraint(memberships.reshape(-1, 128), pltpu.HBM))
    blocks = pl.pallas_call(
        functools.partial(normalise, feat=feat),
        in_specs=[vmem] * 3,
        out_specs=vmem,
        out_shape=f32(sources * lines, 128),
        compiler_params=small,
        name="normalise",
    )(blocks, squares, their_squares)
    blocks = lax.all_to_all(
        blocks.reshape(sources, 1, lines * 128), ("row", "chip"), 0, 0, tiled=True
    ).reshape(-1, 128)

    out = pl.pallas_call(
        centroid_update,
        in_specs=[vmem],
        out_specs=vmem,
        out_shape=f32(feat // (chips * cores), 4096 // n_row),
        scratch_shapes=[pltpu.VMEM((512, 128), jnp.float32)],
        compiler_params=small,
        name="centroid_update",
    )(blocks)
    return out.T


def solution(mesh):
    lm = ("chip", "core")
    inner = Mesh(mesh.devices.reshape(mesh.shape["row"], -1, 2), ("row",) + lm)
    in_specs = (P("row", None), P(lm, None), P(lm, None), P("row"))
    out_specs = P("row", lm)
    return jax.shard_map(
        on_device, mesh=inner, in_specs=in_specs, out_specs=out_specs, check_vma=False
    )
```

```python
import functools

import jax
import jax.numpy as jnp
from jax import lax
from jax.experimental import pallas as pl
from jax.experimental.pallas import tpu as pltpu
from jax.sharding import PartitionSpec as P

LEVELS = 7
F8 = jnp.float8_e4m3fn
CHUNKS = (256, 512, 512, 512, 256)
MIB = 1 << 20


def dot_nt(left, right):
    return lax.dot_general(left, right, (((1,), (1,)), ((), ())), preferred_element_type=jnp.float32)


def partial_features(fp, lm, w, other, own, fp_v, lm_v, w_v, turned_w, shared, row_total, land_total, *rest):
    factors, sem = (rest[0:2], rest[2:4]), rest[4]
    w_copy = pltpu.make_async_copy(w, w_v, sem.at[2 * len(CHUNKS)])
    w_copy.start()
    copies, starts, at = [], [], 0
    for i, width in enumerate(CHUNKS):
        where = (slice(None), pl.ds(at, width))
        pair = (
            pltpu.make_async_copy(fp.at[where], fp_v.at[where], sem.at[2 * i]),
            pltpu.make_async_copy(lm.at[where], lm_v.at[where], sem.at[2 * i + 1]),
        )
        for copy in pair:
            copy.start()
        copies.append(pair)
        starts.append(at)
        at += width
    one, zero = jnp.ones((), jnp.bfloat16), jnp.zeros((), jnp.bfloat16)

    feat = w_v.shape[1]
    half = feat // 2
    column = lax.broadcasted_iota(jnp.int32, (feat, half), 0)
    place = lax.broadcasted_iota(jnp.int32, (feat, half), 1)
    place = feat - 32 - 2 * (place - place % 16) + place % 16
    this = lax.axis_index("lm") % 2
    w_copy.wait()
    for part, core in enumerate((1 - this, this)):
        pick = jnp.where(column == place + 16 * core, 1.0, 0.0).astype(jnp.bfloat16)
        picked = jnp.dot(w_v[...], pick, preferred_element_type=jnp.float32)
        turned_w[:, part * half : (part + 1) * half] = picked.astype(jnp.bfloat16)

    def convert(i):
        width, (left, right) = CHUNKS[i], factors[i % 2]
        for copy in copies[i]:
            copy.wait()
        a = fp_v[:, starts[i] : starts[i] + width].astype(jnp.float32)
        b = lm_v[:, starts[i] : starts[i] + width].astype(jnp.float32).astype(jnp.bfloat16)
        rows = jnp.sum(a, axis=1, keepdims=True)
        lands = dot_nt(jnp.ones((8, width), jnp.bfloat16), b)[:1]
        if i == 0:
            row_total[...], land_total[...] = rows, lands
        else:
            row_total[...] += rows
            land_total[...] += lands
        a = a.astype(jnp.bfloat16)
        for level in range(1, LEVELS + 1):
            t = jnp.bfloat16(level)
            where = slice((level - 1) * width, level * width)
            left[:, where] = (a if level == LEVELS else jnp.minimum(a, t)).astype(F8)
            right[:, where] = jnp.where(b == t, one, zero).astype(F8)

    convert(0)
    for i, width in enumerate(CHUNKS):
        left, right = factors[i % 2]
        part = dot_nt(left[:, : LEVELS * width], right[:, : LEVELS * width])
        if i == 0:
            shared[...] = part
        else:
            shared[...] += part
        if i + 1 < len(CHUNKS):
            convert(i + 1)
    s = shared[...]
    kernel = (s / (row_total[...] + land_total[...] - s)).astype(jnp.bfloat16)
    raw = jnp.dot(kernel, turned_w[...], preferred_element_type=jnp.float32)
    other[...], own[...] = raw[:, :half], raw[:, half:]


def add_theirs(own, theirs, both):
    both[...] = own[...] + theirs[...]


def sum_parts(parts, turned, squares):
    raw = parts[0]
    for i in range(1, parts.shape[0]):
        raw = raw + parts[i]
    rows, half = raw.shape
    raw = jnp.concatenate([raw, jnp.zeros((128 - rows, half), jnp.float32)], 0).T
    turned[...] = raw
    squares[...] = jnp.broadcast_to(jnp.sum(raw * raw, axis=0, keepdims=True), squares.shape)


def lay_out(turned, member, lines):
    owners = turned.shape[0] // 16
    rows, count = 128 // 4, lines.shape[0] - 1
    for h in range(count):
        lines[h] = jnp.concatenate(
            [turned[pl.ds(4 * h + f, owners, stride=16), :][:, :rows] for f in range(4)], 1
        )
    chip = owners - 1 - lax.axis_index("lm") // 2
    line = member[pl.ds(chip // 4, 1), :].astype(jnp.float32)
    line = pltpu.roll(line, 128 - rows * (chip % 4), axis=1)
    lines[count] = jnp.broadcast_to(line, (owners, 128))


def normalise(lines, mine, theirs, out, *, feat):
    count, owners, _ = lines.shape
    rows = 128 // 4
    root = jnp.sqrt((mine[...] + theirs[...])[:1] / feat + 1e-06)
    root = jnp.concatenate([root[:, :rows]] * 4, 1)
    for h in range(count):
        line = lines[h] / root if h + 1 < count else lines[h]
        for z in range(out.shape[0] // (count * owners)):
            out[pl.ds(count * owners * z + h, owners, stride=count), :] = line


def centroid_update(blocks, out, turned):
    count, rows, cents = 5, 32, out.shape[1]
    sources = blocks.shape[0] // count
    for h in range(count - 1):
        turned[pl.ds(128 * h, 128), :] = blocks[pl.ds(h, sources, stride=count), :].T
    label = lax.broadcasted_iota(jnp.int32, (sources, cents), 1)
    local = blocks[pl.ds(count - 1, sources, stride=count), :].astype(jnp.int32) - lax.axis_index("row") * cents
    acc = jnp.zeros((64, cents), jnp.float32)
    for j in range(0, rows, 2):
        both = (j, j + 1)
        value = jnp.concatenate([turned[pl.ds(i, 16, stride=rows), :] for i in both], 1)
        high = value.astype(jnp.bfloat16)
        rest = value - high.astype(jnp.float32)
        mid = rest.astype(jnp.bfloat16)
        low = (rest - mid.astype(jnp.float32)).astype(jnp.bfloat16)
        left = jnp.concatenate([high, mid, low, jnp.ones((16, 2 * sources), jnp.bfloat16)], 0)
        onehot = jnp.concatenate(
            [jnp.where(local[:, i : i + 1] == label, 1.0, 0.0).astype(jnp.bfloat16) for i in both], 0
        )
        acc = acc + jnp.dot(left, onehot, preferred_element_type=jnp.float32)
    sums = acc[0:16] + (acc[16:32] + acc[32:48])
    out[...] = sums / jnp.maximum(acc[48:49], 1.0)


def on_device(fingerprints, landmarks, whitening, memberships):
    rows, width = fingerprints.shape
    lands, feat = whitening.shape
    n_row, n_lm = lax.axis_size("row"), lax.axis_size("lm")
    cores = 2
    chips = n_lm // cores
    half = feat // cores
    owned = rows // chips
    sources, lines = n_row * chips, 5
    swap = [(i, i ^ 1) for i in range(n_lm)]
    plane = [[i for i in reversed(range(n_lm)) if i % cores == k] for k in range(cores)]
    whole = [[i for i in reversed(range(n_row * n_lm)) if i % cores == k] for k in range(cores)]
    hbm, vmem = (pl.BlockSpec(memory_space=m) for m in (pltpu.HBM, pltpu.VMEM))
    factor = pltpu.VMEM((rows, LEVELS * max(CHUNKS)), F8)
    small = pltpu.CompilerParams(vmem_limit_bytes=12 * MIB)

    def f32(*shape):
        return jax.ShapeDtypeStruct(shape, jnp.float32)

    other, own = pl.pallas_call(
        partial_features,
        in_specs=[hbm] * 3,
        out_specs=[vmem, vmem],
        out_shape=[f32(rows, half)] * 2,
        scratch_shapes=[
            pltpu.VMEM((rows, width), jnp.int32),
            pltpu.VMEM((lands, width), jnp.int32),
            pltpu.VMEM((lands, feat), jnp.bfloat16),
            pltpu.VMEM((lands, feat), jnp.bfloat16),
            pltpu.VMEM((rows, lands), jnp.float32),
            pltpu.VMEM((rows, 1), jnp.float32),
            pltpu.VMEM((1, lands), jnp.float32),
            factor, factor, factor, factor,
            pltpu.SemaphoreType.DMA((2 * len(CHUNKS) + 1,)),
        ],
        compiler_params=pltpu.CompilerParams(vmem_limit_bytes=40 * MIB),
        name="partial_features",
    )(
        *(pltpu.with_memory_space_constraint(x, pltpu.HBM) for x in (fingerprints, landmarks, whitening)),
    )

    theirs = lax.ppermute(other, "lm", swap)
    both = pl.pallas_call(
        add_theirs,
        in_specs=[vmem] * 2,
        out_specs=vmem,
        out_shape=f32(rows, half),
        compiler_params=small,
        name="add_theirs",
    )(own, theirs)
    parts = lax.all_to_all(both, "lm", 0, 0, tiled=True, axis_index_groups=plane)

    turned, squares = pl.pallas_call(
        sum_parts,
        in_specs=[vmem],
        out_specs=[vmem] * 2,
        out_shape=[f32(half, 128), f32(8, 128)],
        compiler_params=small,
        name="sum_parts",
    )(parts.reshape(chips, owned, half))
    their_squares = lax.ppermute(squares, "lm", swap)
    blocks = pl.pallas_call(
        lay_out,
        in_specs=[vmem] * 2,
        out_specs=vmem,
        out_shape=f32(lines, chips, 128),
        compiler_params=small,
        name="lay_out",
    )(turned, pltpu.with_memory_space_constraint(memberships.reshape(-1, 128), pltpu.HBM))
    blocks = pl.pallas_call(
        functools.partial(normalise, feat=feat),
        in_specs=[vmem] * 3,
        out_specs=vmem,
        out_shape=f32(sources * lines, 128),
        compiler_params=small,
        name="normalise",
    )(blocks, squares, their_squares)
    blocks = lax.all_to_all(
        blocks.reshape(sources, 1, lines * 128), ("row", "lm"), 0, 0, tiled=True, axis_index_groups=whole
    ).reshape(-1, 128)

    out = pl.pallas_call(
        centroid_update,
        in_specs=[vmem],
        out_specs=vmem,
        out_shape=f32(feat // (chips * cores), 4096 // n_row),
        scratch_shapes=[pltpu.VMEM((512, 128), jnp.float32)],
        compiler_params=small,
        name="centroid_update",
    )(blocks)
    return out.T


def solution(mesh):
    in_specs = (P("row", None), P("lm", None), P("lm", None), P("row"))
    out_specs = P("row", "lm")
    return jax.shard_map(
        on_device, mesh=mesh, in_specs=in_specs, out_specs=out_specs, check_vma=False
    )
```

```python
import functools

import jax
import jax.numpy as jnp
from jax import lax
from jax.experimental import pallas as pl
from jax.experimental.pallas import tpu as pltpu
from jax.sharding import PartitionSpec as P

LEVELS = 7
F8 = jnp.float8_e4m3fn
CHUNKS = (256, 512, 512, 512, 256)
MIB = 1 << 20


def dot_nt(left, right):
    return lax.dot_general(left, right, (((1,), (1,)), ((), ())), preferred_element_type=jnp.float32)


def partial_features(fp, lm, w, other, own, fp_v, lm_v, w_v, turned_w, shared, row_total, land_total, *rest):
    factors, sem = (rest[0:2], rest[2:4]), rest[4]
    w_copy = pltpu.make_async_copy(w, w_v, sem.at[2 * len(CHUNKS)])
    w_copy.start()
    copies, starts, at = [], [], 0
    for i, width in enumerate(CHUNKS):
        where = (slice(None), pl.ds(at, width))
        pair = (
            pltpu.make_async_copy(fp.at[where], fp_v.at[where], sem.at[2 * i]),
            pltpu.make_async_copy(lm.at[where], lm_v.at[where], sem.at[2 * i + 1]),
        )
        for copy in pair:
            copy.start()
        copies.append(pair)
        starts.append(at)
        at += width
    one, zero = jnp.ones((), jnp.bfloat16), jnp.zeros((), jnp.bfloat16)

    feat = w_v.shape[1]
    half = feat // 2
    column = lax.broadcasted_iota(jnp.int32, (feat, half), 0)
    place = lax.broadcasted_iota(jnp.int32, (feat, half), 1)
    place = feat - 32 - 2 * (place - place % 16) + place % 16
    this = lax.axis_index("lm") % 2
    w_copy.wait()
    for part, core in enumerate((1 - this, this)):
        pick = jnp.where(column == place + 16 * core, 1.0, 0.0).astype(jnp.bfloat16)
        picked = jnp.dot(w_v[...], pick, preferred_element_type=jnp.float32)
        turned_w[:, part * half : (part + 1) * half] = picked.astype(jnp.bfloat16)

    def convert(i):
        width, (left, right) = CHUNKS[i], factors[i % 2]
        for copy in copies[i]:
            copy.wait()
        a = fp_v[:, starts[i] : starts[i] + width].astype(jnp.float32)
        b = lm_v[:, starts[i] : starts[i] + width].astype(jnp.float32).astype(jnp.bfloat16)
        rows = jnp.sum(a, axis=1, keepdims=True)
        lands = dot_nt(jnp.ones((8, width), jnp.bfloat16), b)[:1]
        if i == 0:
            row_total[...], land_total[...] = rows, lands
        else:
            row_total[...] += rows
            land_total[...] += lands
        a = a.astype(jnp.bfloat16)
        for level in range(1, LEVELS + 1):
            t = jnp.bfloat16(level)
            where = slice((level - 1) * width, level * width)
            left[:, where] = (a if level == LEVELS else jnp.minimum(a, t)).astype(F8)
            right[:, where] = jnp.where(b == t, one, zero).astype(F8)

    convert(0)
    for i, width in enumerate(CHUNKS):
        left, right = factors[i % 2]
        part = dot_nt(left[:, : LEVELS * width], right[:, : LEVELS * width])
        if i == 0:
            shared[...] = part
        else:
            shared[...] += part
        if i + 1 < len(CHUNKS):
            convert(i + 1)
    s = shared[...]
    kernel = (s / (row_total[...] + land_total[...] - s)).astype(jnp.bfloat16)
    raw = jnp.dot(kernel, turned_w[...], preferred_element_type=jnp.float32)
    other[...], own[...] = raw[:, :half], raw[:, half:]


def add_theirs(own, theirs, both):
    both[...] = own[...] + theirs[...]


def sum_parts(parts, turned, squares):
    raw = parts[0]
    for i in range(1, parts.shape[0]):
        raw = raw + parts[i]
    rows, half = raw.shape
    raw = jnp.concatenate([raw, jnp.zeros((128 - rows, half), jnp.float32)], 0).T
    turned[...] = raw
    squares[...] = jnp.broadcast_to(jnp.sum(raw * raw, axis=0, keepdims=True), squares.shape)


def lay_out(turned, member, lines):
    owners = turned.shape[0] // 16
    rows, count = 128 // 4, lines.shape[0] - 1
    for h in range(count):
        lines[h] = jnp.concatenate(
            [turned[pl.ds(4 * h + f, owners, stride=16), :][:, :rows] for f in range(4)], 1
        )
    chip = owners - 1 - lax.axis_index("lm") // 2
    line = member[pl.ds(chip // 4, 1), :].astype(jnp.float32)
    line = pltpu.roll(line, 128 - rows * (chip % 4), axis=1)
    lines[count] = jnp.broadcast_to(line, (owners, 128))


def normalise(lines, mine, theirs, out, *, feat):
    count, owners, _ = lines.shape
    rows = 128 // 4
    root = jnp.sqrt((mine[...] + theirs[...])[:1] / feat + 1e-06)
    root = jnp.concatenate([root[:, :rows]] * 4, 1)
    for h in range(count):
        line = lines[h] / root if h + 1 < count else lines[h]
        for z in range(out.shape[0] // (count * owners)):
            out[pl.ds(count * owners * z + h, owners, stride=count), :] = line


def centroid_update(blocks, out, turned):
    count, rows, cents = 5, 32, out.shape[1]
    sources = blocks.shape[0] // count
    for h in range(count - 1):
        turned[pl.ds(128 * h, 128), :] = blocks[pl.ds(h, sources, stride=count), :].T
    label = lax.broadcasted_iota(jnp.int32, (sources, cents), 1)
    local = blocks[pl.ds(count - 1, sources, stride=count), :].astype(jnp.int32) - lax.axis_index("row") * cents
    acc = jnp.zeros((64, cents), jnp.float32)
    for j in range(0, rows, 2):
        both = (j, j + 1)
        value = jnp.concatenate([turned[pl.ds(i, 16, stride=rows), :] for i in both], 1)
        high = value.astype(jnp.bfloat16)
        rest = value - high.astype(jnp.float32)
        mid = rest.astype(jnp.bfloat16)
        low = (rest - mid.astype(jnp.float32)).astype(jnp.bfloat16)
        left = jnp.concatenate([high, mid, low, jnp.ones((16, 2 * sources), jnp.bfloat16)], 0)
        onehot = jnp.concatenate(
            [jnp.where(local[:, i : i + 1] == label, 1.0, 0.0).astype(jnp.bfloat16) for i in both], 0
        )
        acc = acc + jnp.dot(left, onehot, preferred_element_type=jnp.float32)
    sums = acc[0:16] + (acc[16:32] + acc[32:48])
    out[...] = sums / jnp.maximum(acc[48:49], 1.0)


def on_device(fingerprints, landmarks, whitening, memberships):
    rows, width = fingerprints.shape
    lands, feat = whitening.shape
    n_row, n_lm = lax.axis_size("row"), lax.axis_size("lm")
    cores = 2
    chips = n_lm // cores
    half = feat // cores
    owned = rows // chips
    sources, lines = n_row * chips, 5
    swap = [(i, i ^ 1) for i in range(n_lm)]
    plane = [[i for i in reversed(range(n_lm)) if i % cores == k] for k in range(cores)]
    order = [z for pair in zip(reversed(range(n_row // 2, n_row)), reversed(range(n_row // 2))) for z in pair]
    whole = [[z * n_lm + i for z in order for i in plane[k]] for k in range(cores)]
    hbm, vmem = (pl.BlockSpec(memory_space=m) for m in (pltpu.HBM, pltpu.VMEM))
    factor = pltpu.VMEM((rows, LEVELS * max(CHUNKS)), F8)
    small = pltpu.CompilerParams(vmem_limit_bytes=12 * MIB)

    def f32(*shape):
        return jax.ShapeDtypeStruct(shape, jnp.float32)

    other, own = pl.pallas_call(
        partial_features,
        in_specs=[hbm] * 3,
        out_specs=[vmem, vmem],
        out_shape=[f32(rows, half)] * 2,
        scratch_shapes=[
            pltpu.VMEM((rows, width), jnp.int32),
            pltpu.VMEM((lands, width), jnp.int32),
            pltpu.VMEM((lands, feat), jnp.bfloat16),
            pltpu.VMEM((lands, feat), jnp.bfloat16),
            pltpu.VMEM((rows, lands), jnp.float32),
            pltpu.VMEM((rows, 1), jnp.float32),
            pltpu.VMEM((1, lands), jnp.float32),
            factor, factor, factor, factor,
            pltpu.SemaphoreType.DMA((2 * len(CHUNKS) + 1,)),
        ],
        compiler_params=pltpu.CompilerParams(vmem_limit_bytes=40 * MIB),
        name="partial_features",
    )(
        *(pltpu.with_memory_space_constraint(x, pltpu.HBM) for x in (fingerprints, landmarks, whitening)),
    )

    theirs = lax.ppermute(other, "lm", swap)
    both = pl.pallas_call(
        add_theirs,
        in_specs=[vmem] * 2,
        out_specs=vmem,
        out_shape=f32(rows, half),
        compiler_params=small,
        name="add_theirs",
    )(own, theirs)
    parts = lax.all_to_all(both, "lm", 0, 0, tiled=True, axis_index_groups=plane)

    turned, squares = pl.pallas_call(
        sum_parts,
        in_specs=[vmem],
        out_specs=[vmem] * 2,
        out_shape=[f32(half, 128), f32(8, 128)],
        compiler_params=small,
        name="sum_parts",
    )(parts.reshape(chips, owned, half))
    their_squares = lax.ppermute(squares, "lm", swap)
    blocks = pl.pallas_call(
        lay_out,
        in_specs=[vmem] * 2,
        out_specs=vmem,
        out_shape=f32(lines, chips, 128),
        compiler_params=small,
        name="lay_out",
    )(turned, pltpu.with_memory_space_constraint(memberships.reshape(-1, 128), pltpu.HBM))
    blocks = pl.pallas_call(
        functools.partial(normalise, feat=feat),
        in_specs=[vmem] * 3,
        out_specs=vmem,
        out_shape=f32(sources * lines, 128),
        compiler_params=small,
        name="normalise",
    )(blocks, squares, their_squares)
    blocks = lax.all_to_all(
        blocks.reshape(sources, 1, lines * 128), ("row", "lm"), 0, 0, tiled=True, axis_index_groups=whole
    ).reshape(-1, 128)

    out = pl.pallas_call(
        centroid_update,
        in_specs=[vmem],
        out_specs=vmem,
        out_shape=f32(feat // (chips * cores), 4096 // n_row),
        scratch_shapes=[pltpu.VMEM((512, 128), jnp.float32)],
        compiler_params=small,
        name="centroid_update",
    )(blocks)
    return out.T


def solution(mesh):
    in_specs = (P("row", None), P("lm", None), P("lm", None), P("row"))
    out_specs = P("row", "lm")
    return jax.shard_map(
        on_device, mesh=mesh, in_specs=in_specs, out_specs=out_specs, check_vma=False
    )
```

```python
import functools

import jax
import jax.numpy as jnp
from jax import lax
from jax.experimental import pallas as pl
from jax.experimental.pallas import tpu as pltpu
from jax.sharding import PartitionSpec as P

LEVELS = 7
F8 = jnp.float8_e4m3fn
CHUNKS = (256, 512, 512, 512, 256)
MIB = 1 << 20


def dot_nt(left, right):
    return lax.dot_general(left, right, (((1,), (1,)), ((), ())), preferred_element_type=jnp.float32)


def partial_features(fp, lm, w, other, own, fp_v, lm_v, w_v, turned_w, shared, row_total, land_total, *rest):
    factors, sem = (rest[0:2], rest[2:4]), rest[4]
    w_copy = pltpu.make_async_copy(w, w_v, sem.at[2 * len(CHUNKS)])
    w_copy.start()
    copies, starts, at = [], [], 0
    for i, width in enumerate(CHUNKS):
        where = (slice(None), pl.ds(at, width))
        pair = (
            pltpu.make_async_copy(fp.at[where], fp_v.at[where], sem.at[2 * i]),
            pltpu.make_async_copy(lm.at[where], lm_v.at[where], sem.at[2 * i + 1]),
        )
        for copy in pair:
            copy.start()
        copies.append(pair)
        starts.append(at)
        at += width
    one, zero = jnp.ones((), jnp.bfloat16), jnp.zeros((), jnp.bfloat16)

    feat = w_v.shape[1]
    half = feat // 2
    column = lax.broadcasted_iota(jnp.int32, (feat, half), 0)
    place = lax.broadcasted_iota(jnp.int32, (feat, half), 1)
    place = feat - 32 - 2 * (place - place % 16) + place % 16
    this = lax.axis_index("lm") % 2
    w_copy.wait()
    for part, core in enumerate((1 - this, this)):
        pick = jnp.where(column == place + 16 * core, 1.0, 0.0).astype(jnp.bfloat16)
        picked = jnp.dot(w_v[...], pick, preferred_element_type=jnp.float32)
        turned_w[:, part * half : (part + 1) * half] = picked.astype(jnp.bfloat16)

    def convert(i):
        width, (left, right) = CHUNKS[i], factors[i % 2]
        for copy in copies[i]:
            copy.wait()
        a = fp_v[:, starts[i] : starts[i] + width].astype(jnp.float32)
        b = lm_v[:, starts[i] : starts[i] + width].astype(jnp.float32).astype(jnp.bfloat16)
        rows = jnp.sum(a, axis=1, keepdims=True)
        lands = dot_nt(jnp.ones((8, width), jnp.bfloat16), b)[:1]
        if i == 0:
            row_total[...], land_total[...] = rows, lands
        else:
            row_total[...] += rows
            land_total[...] += lands
        a = a.astype(jnp.bfloat16)
        for level in range(1, LEVELS + 1):
            t = jnp.bfloat16(level)
            where = slice((level - 1) * width, level * width)
            left[:, where] = (a if level == LEVELS else jnp.minimum(a, t)).astype(F8)
            right[:, where] = jnp.where(b == t, one, zero).astype(F8)

    convert(0)
    for i, width in enumerate(CHUNKS):
        left, right = factors[i % 2]
        part = dot_nt(left[:, : LEVELS * width], right[:, : LEVELS * width])
        if i == 0:
            shared[...] = part
        else:
            shared[...] += part
        if i + 1 < len(CHUNKS):
            convert(i + 1)
    s = shared[...]
    kernel = (s / (row_total[...] + land_total[...] - s)).astype(jnp.bfloat16)
    raw = jnp.dot(kernel, turned_w[...], preferred_element_type=jnp.float32)
    other[...], own[...] = raw[:, :half], raw[:, half:]


def add_theirs(own, theirs, both):
    both[...] = own[...] + theirs[...]


def sum_parts(parts, turned, squares):
    raw = parts[0]
    for i in range(1, parts.shape[0]):
        raw = raw + parts[i]
    rows, half = raw.shape
    raw = jnp.concatenate([raw, jnp.zeros((128 - rows, half), jnp.float32)], 0).T
    turned[...] = raw
    squares[...] = jnp.broadcast_to(jnp.sum(raw * raw, axis=0, keepdims=True), squares.shape)


def lay_out(turned, member, lines):
    owners = turned.shape[0] // 16
    rows, count = 128 // 4, lines.shape[0] - 1
    for h in range(count):
        lines[h] = jnp.concatenate(
            [turned[pl.ds(4 * h + f, owners, stride=16), :][:, :rows] for f in range(4)], 1
        )
    back = owners - 1 - lax.axis_index("lm") // 2
    chip = 2 * (back % (owners // 2)) + back // (owners // 2)
    line = member[pl.ds(chip // 4, 1), :].astype(jnp.float32)
    line = pltpu.roll(line, 128 - rows * (chip % 4), axis=1)
    lines[count] = jnp.broadcast_to(line, (owners, 128))


def normalise(lines, mine, theirs, out, *, feat):
    count, owners, _ = lines.shape
    rows = 128 // 4
    root = jnp.sqrt((mine[...] + theirs[...])[:1] / feat + 1e-06)
    root = jnp.concatenate([root[:, :rows]] * 4, 1)
    for h in range(count):
        line = lines[h] / root if h + 1 < count else lines[h]
        for z in range(out.shape[0] // (count * owners)):
            out[pl.ds(count * owners * z + h, owners, stride=count), :] = line


def centroid_update(blocks, out, turned):
    count, rows, cents = 5, 32, out.shape[1]
    sources = blocks.shape[0] // count
    for h in range(count - 1):
        turned[pl.ds(128 * h, 128), :] = blocks[pl.ds(h, sources, stride=count), :].T
    label = lax.broadcasted_iota(jnp.int32, (sources, cents), 1)
    local = blocks[pl.ds(count - 1, sources, stride=count), :].astype(jnp.int32) - lax.axis_index("row") * cents
    acc = jnp.zeros((64, cents), jnp.float32)
    for j in range(0, rows, 2):
        both = (j, j + 1)
        value = jnp.concatenate([turned[pl.ds(i, 16, stride=rows), :] for i in both], 1)
        high = value.astype(jnp.bfloat16)
        rest = value - high.astype(jnp.float32)
        mid = rest.astype(jnp.bfloat16)
        low = (rest - mid.astype(jnp.float32)).astype(jnp.bfloat16)
        left = jnp.concatenate([high, mid, low, jnp.ones((16, 2 * sources), jnp.bfloat16)], 0)
        onehot = jnp.concatenate(
            [jnp.where(local[:, i : i + 1] == label, 1.0, 0.0).astype(jnp.bfloat16) for i in both], 0
        )
        acc = acc + jnp.dot(left, onehot, preferred_element_type=jnp.float32)
    sums = acc[0:16] + (acc[16:32] + acc[32:48])
    out[...] = sums / jnp.maximum(acc[48:49], 1.0)


def on_device(fingerprints, landmarks, whitening, memberships):
    rows, width = fingerprints.shape
    lands, feat = whitening.shape
    n_row, n_lm = lax.axis_size("row"), lax.axis_size("lm")
    cores = 2
    chips = n_lm // cores
    half = feat // cores
    owned = rows // chips
    sources, lines = n_row * chips, 5
    swap = [(i, i ^ 1) for i in range(n_lm)]
    plane = [[i for i in reversed(range(n_lm)) if i % cores == k] for k in range(cores)]
    turns = [[p[i // 2 + (i % 2) * (chips // 2)] for i in range(chips)] for p in plane]
    order = [z for pair in zip(reversed(range(n_row // 2, n_row)), reversed(range(n_row // 2))) for z in pair]
    whole = [[z * n_lm + i for z in order for i in plane[k]] for k in range(cores)]
    hbm, vmem = (pl.BlockSpec(memory_space=m) for m in (pltpu.HBM, pltpu.VMEM))
    factor = pltpu.VMEM((rows, LEVELS * max(CHUNKS)), F8)
    small = pltpu.CompilerParams(vmem_limit_bytes=12 * MIB)

    def f32(*shape):
        return jax.ShapeDtypeStruct(shape, jnp.float32)

    other, own = pl.pallas_call(
        partial_features,
        in_specs=[hbm] * 3,
        out_specs=[vmem, vmem],
        out_shape=[f32(rows, half)] * 2,
        scratch_shapes=[
            pltpu.VMEM((rows, width), jnp.int32),
            pltpu.VMEM((lands, width), jnp.int32),
            pltpu.VMEM((lands, feat), jnp.bfloat16),
            pltpu.VMEM((lands, feat), jnp.bfloat16),
            pltpu.VMEM((rows, lands), jnp.float32),
            pltpu.VMEM((rows, 1), jnp.float32),
            pltpu.VMEM((1, lands), jnp.float32),
            factor, factor, factor, factor,
            pltpu.SemaphoreType.DMA((2 * len(CHUNKS) + 1,)),
        ],
        compiler_params=pltpu.CompilerParams(vmem_limit_bytes=40 * MIB),
        name="partial_features",
    )(
        *(pltpu.with_memory_space_constraint(x, pltpu.HBM) for x in (fingerprints, landmarks, whitening)),
    )

    theirs = lax.ppermute(other, "lm", swap)
    both = pl.pallas_call(
        add_theirs,
        in_specs=[vmem] * 2,
        out_specs=vmem,
        out_shape=f32(rows, half),
        compiler_params=small,
        name="add_theirs",
    )(own, theirs)
    parts = lax.all_to_all(both, "lm", 0, 0, tiled=True, axis_index_groups=turns)

    turned, squares = pl.pallas_call(
        sum_parts,
        in_specs=[vmem],
        out_specs=[vmem] * 2,
        out_shape=[f32(half, 128), f32(8, 128)],
        compiler_params=small,
        name="sum_parts",
    )(parts.reshape(chips, owned, half))
    their_squares = lax.ppermute(squares, "lm", swap)
    blocks = pl.pallas_call(
        lay_out,
        in_specs=[vmem] * 2,
        out_specs=vmem,
        out_shape=f32(lines, chips, 128),
        compiler_params=small,
        name="lay_out",
    )(turned, pltpu.with_memory_space_constraint(memberships.reshape(-1, 128), pltpu.HBM))
    blocks = pl.pallas_call(
        functools.partial(normalise, feat=feat),
        in_specs=[vmem] * 3,
        out_specs=vmem,
        out_shape=f32(sources * lines, 128),
        compiler_params=small,
        name="normalise",
    )(blocks, squares, their_squares)
    blocks = lax.all_to_all(
        blocks.reshape(sources, 1, lines * 128), ("row", "lm"), 0, 0, tiled=True, axis_index_groups=whole
    ).reshape(-1, 128)

    out = pl.pallas_call(
        centroid_update,
        in_specs=[vmem],
        out_specs=vmem,
        out_shape=f32(feat // (chips * cores), 4096 // n_row),
        scratch_shapes=[pltpu.VMEM((512, 128), jnp.float32)],
        compiler_params=small,
        name="centroid_update",
    )(blocks)
    return out.T


def solution(mesh):
    in_specs = (P("row", None), P("lm", None), P("lm", None), P("row"))
    out_specs = P("row", "lm")
    return jax.shard_map(
        on_device, mesh=mesh, in_specs=in_specs, out_specs=out_specs, check_vma=False
    )
```

```python
import functools

import jax
import jax.numpy as jnp
from jax import lax
from jax.experimental import pallas as pl
from jax.experimental.pallas import tpu as pltpu
from jax.sharding import PartitionSpec as P

LEVELS = 7
F8 = jnp.float8_e4m3fn
CHUNKS = (256, 512, 512, 512, 256)
MIB = 1 << 20


def dot_nt(left, right):
    return lax.dot_general(left, right, (((1,), (1,)), ((), ())), preferred_element_type=jnp.float32)


def partial_features(fp, lm, w, other, own, fp_v, lm_v, w_v, turned_w, shared, row_total, land_total, *rest):
    factors, sem = (rest[0:2], rest[2:4]), rest[4]
    w_copy = pltpu.make_async_copy(w, w_v, sem.at[2 * len(CHUNKS)])
    w_copy.start()
    copies, starts, at = [], [], 0
    for i, width in enumerate(CHUNKS):
        where = (slice(None), pl.ds(at, width))
        pair = (
            pltpu.make_async_copy(fp.at[where], fp_v.at[where], sem.at[2 * i]),
            pltpu.make_async_copy(lm.at[where], lm_v.at[where], sem.at[2 * i + 1]),
        )
        for copy in pair:
            copy.start()
        copies.append(pair)
        starts.append(at)
        at += width
    one, zero = jnp.ones((), jnp.bfloat16), jnp.zeros((), jnp.bfloat16)

    feat = w_v.shape[1]
    half = feat // 2
    column = lax.broadcasted_iota(jnp.int32, (feat, half), 0)
    place = lax.broadcasted_iota(jnp.int32, (feat, half), 1)
    place = feat - 32 - 2 * (place - place % 16) + place % 16
    this = lax.axis_index("lm") % 2
    w_copy.wait()
    for part, core in enumerate((1 - this, this)):
        pick = jnp.where(column == place + 16 * core, 1.0, 0.0).astype(jnp.bfloat16)
        picked = jnp.dot(w_v[...], pick, preferred_element_type=jnp.float32)
        turned_w[:, part * half : (part + 1) * half] = picked.astype(jnp.bfloat16)

    def convert(i):
        width, (left, right) = CHUNKS[i], factors[i % 2]
        for copy in copies[i]:
            copy.wait()
        a = fp_v[:, starts[i] : starts[i] + width].astype(jnp.float32)
        b = lm_v[:, starts[i] : starts[i] + width].astype(jnp.float32).astype(jnp.bfloat16)
        rows = jnp.sum(a, axis=1, keepdims=True)
        lands = dot_nt(jnp.ones((8, width), jnp.bfloat16), b)[:1]
        if i == 0:
            row_total[...], land_total[...] = rows, lands
        else:
            row_total[...] += rows
            land_total[...] += lands
        a = a.astype(jnp.bfloat16)
        for level in range(1, LEVELS + 1):
            t = jnp.bfloat16(level)
            where = slice((level - 1) * width, level * width)
            left[:, where] = (a if level == LEVELS else jnp.minimum(a, t)).astype(F8)
            right[:, where] = jnp.where(b == t, one, zero).astype(F8)

    convert(0)
    for i, width in enumerate(CHUNKS):
        left, right = factors[i % 2]
        part = dot_nt(left[:, : LEVELS * width], right[:, : LEVELS * width])
        if i == 0:
            shared[...] = part
        else:
            shared[...] += part
        if i + 1 < len(CHUNKS):
            convert(i + 1)
    s = shared[...]
    kernel = (s / (row_total[...] + land_total[...] - s)).astype(jnp.bfloat16)
    raw = jnp.dot(kernel, turned_w[...], preferred_element_type=jnp.float32)
    other[...], own[...] = raw[:, :half], raw[:, half:]


def add_theirs(own, theirs, both):
    both[...] = own[...] + theirs[...]


def sum_parts(parts, turned, squares):
    raw = parts[0]
    for i in range(1, parts.shape[0]):
        raw = raw + parts[i]
    rows, half = raw.shape
    raw = jnp.concatenate([raw, jnp.zeros((128 - rows, half), jnp.float32)], 0).T
    turned[...] = raw
    squares[...] = jnp.broadcast_to(jnp.sum(raw * raw, axis=0, keepdims=True), squares.shape)


def lay_out(turned, member, lines):
    owners = turned.shape[0] // 16
    rows, count = 128 // 4, lines.shape[0] - 1
    for h in range(count):
        lines[h] = jnp.concatenate(
            [turned[pl.ds(4 * h + f, owners, stride=16), :][:, :rows] for f in range(4)], 1
        )
    back = owners - 1 - lax.axis_index("lm") // 2
    chip = 8 * (back % 2) + 4 * (back // 2 % 2) + 2 * (back // 4 % 2) + back // 8
    line = member[pl.ds(chip // 4, 1), :].astype(jnp.float32)
    line = pltpu.roll(line, 128 - rows * (chip % 4), axis=1)
    lines[count] = jnp.broadcast_to(line, (owners, 128))


def normalise(lines, mine, theirs, out, *, feat):
    count, owners, _ = lines.shape
    rows = 128 // 4
    root = jnp.sqrt((mine[...] + theirs[...])[:1] / feat + 1e-06)
    root = jnp.concatenate([root[:, :rows]] * 4, 1)
    for h in range(count):
        line = lines[h] / root if h + 1 < count else lines[h]
        for z in range(out.shape[0] // (count * owners)):
            out[pl.ds(count * owners * z + h, owners, stride=count), :] = line


def centroid_update(blocks, out, turned):
    count, rows, cents = 5, 32, out.shape[1]
    sources = blocks.shape[0] // count
    for h in range(count - 1):
        turned[pl.ds(128 * h, 128), :] = blocks[pl.ds(h, sources, stride=count), :].T
    label = lax.broadcasted_iota(jnp.int32, (sources, cents), 1)
    local = blocks[pl.ds(count - 1, sources, stride=count), :].astype(jnp.int32) - lax.axis_index("row") * cents
    acc = jnp.zeros((64, cents), jnp.float32)
    for j in range(0, rows, 2):
        both = (j, j + 1)
        value = jnp.concatenate([turned[pl.ds(i, 16, stride=rows), :] for i in both], 1)
        high = value.astype(jnp.bfloat16)
        rest = value - high.astype(jnp.float32)
        mid = rest.astype(jnp.bfloat16)
        low = (rest - mid.astype(jnp.float32)).astype(jnp.bfloat16)
        left = jnp.concatenate([high, mid, low, jnp.ones((16, 2 * sources), jnp.bfloat16)], 0)
        onehot = jnp.concatenate(
            [jnp.where(local[:, i : i + 1] == label, 1.0, 0.0).astype(jnp.bfloat16) for i in both], 0
        )
        acc = acc + jnp.dot(left, onehot, preferred_element_type=jnp.float32)
    sums = acc[0:16] + (acc[16:32] + acc[32:48])
    out[...] = sums / jnp.maximum(acc[48:49], 1.0)


def on_device(fingerprints, landmarks, whitening, memberships):
    rows, width = fingerprints.shape
    lands, feat = whitening.shape
    n_row, n_lm = lax.axis_size("row"), lax.axis_size("lm")
    cores = 2
    chips = n_lm // cores
    half = feat // cores
    owned = rows // chips
    sources, lines = n_row * chips, 5
    swap = [(i, i ^ 1) for i in range(n_lm)]
    plane = [[i for i in reversed(range(n_lm)) if i % cores == k] for k in range(cores)]
    turns = [[p[8 * (i % 2) + 4 * (i // 2 % 2) + 2 * (i // 4 % 2) + i // 8] for i in range(chips)] for p in plane]
    order = [z for pair in zip(reversed(range(n_row // 2, n_row)), reversed(range(n_row // 2))) for z in pair]
    whole = [[z * n_lm + i for z in order for i in plane[k]] for k in range(cores)]
    hbm, vmem = (pl.BlockSpec(memory_space=m) for m in (pltpu.HBM, pltpu.VMEM))
    factor = pltpu.VMEM((rows, LEVELS * max(CHUNKS)), F8)
    small = pltpu.CompilerParams(vmem_limit_bytes=12 * MIB)

    def f32(*shape):
        return jax.ShapeDtypeStruct(shape, jnp.float32)

    other, own = pl.pallas_call(
        partial_features,
        in_specs=[hbm] * 3,
        out_specs=[vmem, vmem],
        out_shape=[f32(rows, half)] * 2,
        scratch_shapes=[
            pltpu.VMEM((rows, width), jnp.int32),
            pltpu.VMEM((lands, width), jnp.int32),
            pltpu.VMEM((lands, feat), jnp.bfloat16),
            pltpu.VMEM((lands, feat), jnp.bfloat16),
            pltpu.VMEM((rows, lands), jnp.float32),
            pltpu.VMEM((rows, 1), jnp.float32),
            pltpu.VMEM((1, lands), jnp.float32),
            factor, factor, factor, factor,
            pltpu.SemaphoreType.DMA((2 * len(CHUNKS) + 1,)),
        ],
        compiler_params=pltpu.CompilerParams(vmem_limit_bytes=40 * MIB),
        name="partial_features",
    )(
        *(pltpu.with_memory_space_constraint(x, pltpu.HBM) for x in (fingerprints, landmarks, whitening)),
    )

    theirs = lax.ppermute(other, "lm", swap)
    both = pl.pallas_call(
        add_theirs,
        in_specs=[vmem] * 2,
        out_specs=vmem,
        out_shape=f32(rows, half),
        compiler_params=small,
        name="add_theirs",
    )(own, theirs)
    parts = lax.all_to_all(both, "lm", 0, 0, tiled=True, axis_index_groups=turns)

    turned, squares = pl.pallas_call(
        sum_parts,
        in_specs=[vmem],
        out_specs=[vmem] * 2,
        out_shape=[f32(half, 128), f32(8, 128)],
        compiler_params=small,
        name="sum_parts",
    )(parts.reshape(chips, owned, half))
    their_squares = lax.ppermute(squares, "lm", swap)
    blocks = pl.pallas_call(
        lay_out,
        in_specs=[vmem] * 2,
        out_specs=vmem,
        out_shape=f32(lines, chips, 128),
        compiler_params=small,
        name="lay_out",
    )(turned, pltpu.with_memory_space_constraint(memberships.reshape(-1, 128), pltpu.HBM))
    blocks = pl.pallas_call(
        functools.partial(normalise, feat=feat),
        in_specs=[vmem] * 3,
        out_specs=vmem,
        out_shape=f32(sources * lines, 128),
        compiler_params=small,
        name="normalise",
    )(blocks, squares, their_squares)
    blocks = lax.all_to_all(
        blocks.reshape(sources, 1, lines * 128), ("row", "lm"), 0, 0, tiled=True, axis_index_groups=whole
    ).reshape(-1, 128)

    out = pl.pallas_call(
        centroid_update,
        in_specs=[vmem],
        out_specs=vmem,
        out_shape=f32(feat // (chips * cores), 4096 // n_row),
        scratch_shapes=[pltpu.VMEM((512, 128), jnp.float32)],
        compiler_params=small,
        name="centroid_update",
    )(blocks)
    return out.T


def solution(mesh):
    in_specs = (P("row", None), P("lm", None), P("lm", None), P("row"))
    out_specs = P("row", "lm")
    return jax.shard_map(
        on_device, mesh=mesh, in_specs=in_specs, out_specs=out_specs, check_vma=False
    )
```
